32 devices in a mesh: fsdp: 8 (over z, y), tp: 4 (over x, core).
Axes of the slice: x: 2, y: 2, z: 4, core: 2. Of those that a mesh axis runs over, the one named last changes fastest.
Arguments:
- token_ids: int32 [32, 4], replicated, may hold values from 0 to 76031
- lengths: int32 [32], P('fsdp'), may hold values from 64 to 4096, as said below
- embedding: bfloat16 [76032, 8192], P('tp', 'fsdp'), may hold values from -6 to 6
- norm_gain: float32 [8192], replicated, may hold values from 0.1 to 1.9
- w_query: bfloat16 [8192, 4096], P(('fsdp', 'tp')), may hold values from -0.0625 to 0.0625
- w_keyval: bfloat16 [8192, 1024], P(('fsdp', 'tp')), may hold values from -0.15625 to 0.15625
- w_out: bfloat16 [8192, 4096], P(('fsdp', 'tp')), may hold values from -0.09375 to 0.09375
- key_cache: bfloat16 [32, 4096, 512], P('fsdp', None, 'tp'), may hold values from -200 to 200
- value_cache: bfloat16 [32, 4096, 512], P('fsdp', None, 'tp'), may hold values from -15 to 15
Outputs:
- attn_out: bfloat16 [32, 4, 8192], P('fsdp', None, 'tp')
The draws below stay inside these ranges and needn't reach their ends.
Inputs may be any that keep to these rules, and one draw needn't show every extreme that they name: `lengths`: at least one row has 4096 filled slots and at least one has 64.
All inputs are finite; a program needn't handle non-finite values.
Results may differ from the reference program's by a relative error of at most 0.012.
Values may be sent and summed in bfloat16 or wider, within the bound.
A program may use at most 192 MiB of HBM per device.

```python
import math
import jax
import jax.numpy as jnp
import numpy as np
from jax import lax

D = 8192
HD = 128
QH = 32
KVH = 4
VOCAB = 76032
CTX = 4096
STEPS = 4
ROWS = 32


def draw_lengths(key, part):
    key = jax.random.fold_in(key, 11)
    first_key, second_key, third_key = jax.random.split(key, 3)
    drawn = jax.random.randint(first_key, (ROWS,), CTX // 64, CTX + 1)
    longest = jax.random.randint(second_key, (), 0, ROWS)
    offset_row = jax.random.randint(third_key, (), 1, ROWS)
    shortest = (longest + offset_row) % ROWS
    places = jnp.arange(ROWS)
    drawn = jnp.where(places == longest, CTX, drawn)
    drawn = jnp.where(places == shortest, CTX // 64, drawn)
    return drawn.astype(jnp.int32)


def draw_key_cache(key, part):
    key = jax.random.fold_in(key, 23)
    main_key = jax.random.fold_in(key, 0)
    full_shape = (ROWS, CTX, KVH * HD)
    values = jnp.clip(jax.random.normal(main_key, full_shape, jnp.float32), -6.0, 6.0) * 2.5
    return values.astype(jnp.bfloat16)


def plant(values, stream_key, smallest, top_value):
    spot = [jax.random.randint(jax.random.fold_in(stream_key, axis), (), 0, length) for axis, length in enumerate(values.shape)]
    widest = values.shape.index(max(values.shape))
    beside = spot[:widest] + [(spot[widest] + 1) % values.shape[widest]] + spot[widest + 1:]
    return values.at[tuple(spot)].set(smallest).at[tuple(beside)].set(top_value)


def block_levels(stream_key, extent, shards, low, high):
    def one(dim, shards_of):
        steps = jax.random.uniform(jax.random.fold_in(jax.random.fold_in(stream_key, 6), dim), (shards_of,), jnp.float32, low / len(shards), high / len(shards))
        return jnp.repeat(jnp.exp(steps), extent[dim] // shards_of).reshape((-1,) + (1,) * (len(extent) - dim - 1))

    level = one(*shards[0])
    for cut in shards[1:]:
        level = level * one(*cut)
    return level


def skewed_wide(stream_key, shape, count, lean):
    portions = [min(1 << octave, count + 1 - (1 << octave)) * (1 << 20) // math.isqrt((1 << octave) ** lean) + 1 for octave in range((count + 1).bit_length()) if 1 << octave <= count]
    deviation = 1 + sum(portions) // (1 << 30)
    listing = np.cumsum(np.array([max(1, weight // deviation) for weight in portions]))
    pick = jax.random.randint(jax.random.fold_in(stream_key, 1), shape, 0, int(listing[len(portions) - 1]))
    start = jnp.left_shift(1, jnp.searchsorted(jnp.asarray(listing, jnp.int32), pick, side="right").astype(jnp.int32))
    grade = start - 1 + jax.random.randint(jax.random.fold_in(stream_key, 4), shape, 0, 1 << 30) % jnp.minimum(start, count + 1 - start)
    return jax.random.permutation(jax.random.fold_in(stream_key, 2), count)[grade].astype(jnp.int32)


def normal_values(key, dims, spread, bound, cuts=(), kind=jnp.bfloat16):
    entries = spread * jax.random.normal(key, dims, jnp.float32)
    if cuts:
        entries = entries * block_levels(key, dims, cuts, -0.22, 0.18)
    return jnp.clip(entries, -bound, bound).astype(kind)


def setup_inputs(seed: int = 0) -> dict:
    key_of = jax.random.split(jax.random.key(seed), 10)
    return {
        "token_ids": plant(skewed_wide(key_of[0], (ROWS, STEPS), VOCAB, 2), jax.random.fold_in(key_of[0], 3), 0, VOCAB - 1).astype(jnp.int32),
        "lengths": draw_lengths(jax.random.fold_in(key_of[9], 71), 0),
        "embedding": normal_values(key_of[2], (VOCAB, D), 1.0, 6.0, ((0, 4), (1, 8))),
        "norm_gain": jnp.clip(1.0 + 0.18 * jax.random.normal(key_of[3], (D,), jnp.float32), 0.1, 1.9),
        "w_query": normal_values(key_of[4], (D, QH * HD), D ** -0.5, 0.0625, ((0, 32),)),
        "w_keyval": normal_values(key_of[5], (D, KVH * 2 * HD), (D // 6) ** -0.5, 0.15625, ((0, 32),)),
        "w_out": normal_values(key_of[6], (D, QH * HD), (QH * HD) ** -0.5, 0.09375, ((0, 32),)),
        "key_cache": draw_key_cache(jax.random.fold_in(key_of[9], 71), 0),
        "value_cache": normal_values(key_of[8], (ROWS, CTX, KVH * HD), 2.5, 15.0, ((0, 8), (2, 4))),
    }


EPS_NORM = 1e-06
ROPE_BASE = 1000000.0

def rotate(vectors, positions):
    midpoint = vectors.shape[-1] // 2
    frequency = ROPE_BASE ** (-2.0 * jnp.arange(midpoint, dtype=jnp.float32) / vectors.shape[-1])
    angles = positions.astype(jnp.float32)[..., None, None] * frequency
    cosine = jnp.cos(angles)
    sine_part = jnp.sin(angles)
    leading = vectors[..., :midpoint]
    trailing = vectors[..., midpoint:]
    return jnp.concatenate([leading * cosine - trailing * sine_part, trailing * cosine + leading * sine_part], -1)

def reference(token_ids, lengths, embedding, norm_gain, w_query, w_keyval, w_out, key_cache, value_cache):
    inputs = embedding[token_ids].astype(jnp.float32)
    scale_rows = lax.rsqrt(lax.optimization_barrier(jnp.mean(inputs * inputs, -1, keepdims=True)) + EPS_NORM)
    normed = (inputs * scale_rows * norm_gain).astype(jnp.bfloat16).reshape(ROWS * STEPS, D)
    query_proj = jnp.dot(normed, w_query, preferred_element_type=jnp.float32).reshape(ROWS, STEPS, QH, HD)
    keyval_proj = jnp.dot(normed, w_keyval, preferred_element_type=jnp.float32).reshape(ROWS, STEPS, KVH, 2, HD)
    positions = lengths[:, None] + jnp.arange(STEPS, dtype=jnp.int32)[None, :]
    queries = rotate(query_proj, positions).astype(jnp.bfloat16)
    new_keys = rotate(keyval_proj[:, :, :, 0, :], positions).astype(jnp.bfloat16)
    new_values = keyval_proj[:, :, :, 1, :].astype(jnp.bfloat16)
    group_size = QH // KVH
    score_scale = 1.0 / math.sqrt(HD)

    def one_row(packed):
        query_row, key_new, value_new, key_old, value_old, length_row = packed
        all_keys = jnp.concatenate([key_old.reshape(CTX, KVH, HD), key_new], 0).astype(jnp.float32)
        all_values = jnp.concatenate([value_old.reshape(CTX, KVH, HD), value_new], 0).astype(jnp.float32)
        grouped = query_row.reshape(STEPS, KVH, group_size, HD).astype(jnp.float32)
        scores = jnp.einsum('sghd,jgd->sghj', grouped, all_keys) * score_scale
        places = jnp.arange(CTX + STEPS, dtype=jnp.int32)[None, :]
        step_ids = jnp.arange(STEPS, dtype=jnp.int32)[:, None]
        visible = jnp.where(places < CTX, places < length_row, places - CTX <= step_ids)
        visible = visible[:, None, None, :]
        largest = lax.optimization_barrier(jnp.max(jnp.where(visible, scores, -jnp.inf), -1, keepdims=True))
        weights = jnp.where(visible, jnp.exp(scores - largest), 0.0)
        weights = (weights / lax.optimization_barrier(jnp.sum(weights, -1, keepdims=True))).astype(jnp.bfloat16)
        blended = jnp.einsum('sghj,jgd->sghd', weights.astype(jnp.float32), all_values)
        return blended.astype(jnp.bfloat16).reshape(STEPS, QH * HD)
    attended = lax.map(one_row, (queries, new_keys, new_values, key_cache, value_cache, lengths))
    output = jnp.dot(attended.reshape(ROWS * STEPS, QH * HD), w_out.T, preferred_element_type=jnp.float32)
    return output.astype(jnp.bfloat16).reshape(ROWS, STEPS, D)
```

```python
import math

import jax
import jax.numpy as jnp
from jax import lax
from jax.sharding import PartitionSpec as P

HD = 128


EPS_NORM = 1e-06
ROPE_BASE = 1000000.0


def rotate(vectors, positions):
    midpoint = vectors.shape[-1] // 2
    frequency = ROPE_BASE ** (-2.0 * jnp.arange(midpoint, dtype=jnp.float32) / vectors.shape[-1])
    angles = positions.astype(jnp.float32)[..., None, None] * frequency
    cosine = jnp.cos(angles)
    sine_part = jnp.sin(angles)
    leading = vectors[..., :midpoint]
    trailing = vectors[..., midpoint:]
    return jnp.concatenate(
        [leading * cosine - trailing * sine_part, trailing * cosine + leading * sine_part], -1
    )


def contract_last(left, right):
    return lax.dot_general(
        left, right, (((1,), (1,)), ((), ())), preferred_element_type=jnp.float32
    )


def attend(proj_q, proj_kv, lengths, key_cache, value_cache, step_count):
    row_dev = lengths.shape[0]
    context = key_cache.shape[1]
    positions = (lengths[:, None] + jnp.arange(step_count, dtype=jnp.int32)[None, :]).reshape(-1)
    queries = rotate(proj_q.reshape(row_dev * step_count, -1, HD), positions).astype(jnp.bfloat16)
    paired = proj_kv.reshape(row_dev * step_count, -1, 2, HD)
    new_keys = rotate(paired[:, :, 0, :], positions).astype(jnp.bfloat16)
    new_values = paired[:, :, 1, :].astype(jnp.bfloat16)
    kv_heads = key_cache.shape[2] // HD
    group_size = queries.shape[1] // kv_heads
    grouped = queries.reshape(row_dev, step_count, kv_heads, group_size, HD)
    old_keys = key_cache.reshape(row_dev, context, kv_heads, HD)
    old_values = value_cache.reshape(row_dev, context, kv_heads, HD)
    fresh_keys = new_keys.reshape(row_dev, step_count, kv_heads, HD)
    fresh_values = new_values.reshape(row_dev, step_count, kv_heads, HD)
    score_scale = 1.0 / math.sqrt(HD)
    old_scores = (
        jnp.einsum("rsghd,rjgd->rsghj", grouped, old_keys, preferred_element_type=jnp.float32)
        * score_scale
    )
    new_scores = (
        jnp.einsum("rsghd,rtgd->rsght", grouped, fresh_keys, preferred_element_type=jnp.float32)
        * score_scale
    )
    old_seen = (jnp.arange(context, dtype=jnp.int32)[None, :] < lengths[:, None])[
        :, None, None, None, :
    ]
    step_ids = jnp.arange(step_count, dtype=jnp.int32)
    new_seen = (step_ids[None, :] <= step_ids[:, None])[None, :, None, None, :]
    largest = jnp.maximum(
        jnp.max(jnp.where(old_seen, old_scores, -jnp.inf), -1, keepdims=True),
        jnp.max(jnp.where(new_seen, new_scores, -jnp.inf), -1, keepdims=True),
    )
    old_weights = jnp.where(old_seen, jnp.exp(old_scores - largest), 0.0)
    new_weights = jnp.where(new_seen, jnp.exp(new_scores - largest), 0.0)
    totals = jnp.sum(old_weights, -1, keepdims=True) + jnp.sum(new_weights, -1, keepdims=True)
    old_probs = (old_weights / totals).astype(jnp.bfloat16)
    new_probs = (new_weights / totals).astype(jnp.bfloat16)
    blended = jnp.einsum(
        "rsghj,rjgd->rsghd", old_probs, old_values, preferred_element_type=jnp.float32
    )
    blended = blended + jnp.einsum(
        "rsght,rtgd->rsghd", new_probs, fresh_values, preferred_element_type=jnp.float32
    )
    return blended.astype(jnp.bfloat16).reshape(row_dev * step_count, -1)


def on_device(
    token_ids, lengths, embedding, norm_gain, w_query, w_keyval, w_out, key_cache, value_cache
):
    tp_count = lax.axis_size("tp")
    fsdp_count = lax.axis_size("fsdp")
    tp_rank = lax.axis_index("tp")
    fsdp_rank = lax.axis_index("fsdp")
    step_count = token_ids.shape[1]
    row_dev = lengths.shape[0]
    vocab_part = embedding.shape[0]
    token_count = token_ids.size
    depth = w_query.shape[0]
    width = norm_gain.shape[0]
    shifted = token_ids.reshape(-1) - tp_rank * vocab_part
    inside = (shifted >= 0) & (shifted < vocab_part)
    picked = jnp.take(embedding, jnp.clip(shifted, 0, vocab_part - 1), axis=0)
    picked = jnp.where(inside[:, None], picked, jnp.zeros_like(picked))
    parts = lax.all_to_all(
        picked.reshape(token_count, tp_count, depth), "tp", split_axis=1, concat_axis=1, tiled=True
    )
    inputs = jnp.sum(parts.astype(jnp.float32), axis=1)
    gain = lax.dynamic_slice(norm_gain, ((fsdp_rank * tp_count + tp_rank) * depth,), (depth,))
    squares = lax.psum(jnp.sum(inputs * inputs, -1, keepdims=True), ("fsdp", "tp"))
    scale_rows = lax.rsqrt(squares / width + EPS_NORM)
    normed = (inputs * scale_rows * gain).astype(jnp.bfloat16)
    part_q = jnp.dot(normed, w_query, preferred_element_type=jnp.float32)
    part_kv = jnp.dot(normed, w_keyval, preferred_element_type=jnp.float32)
    parts = jnp.concatenate(
        [part_q.reshape(token_count, tp_count, -1), part_kv.reshape(token_count, tp_count, -1)], -1
    )
    mine = lax.psum_scatter(parts, "tp", scatter_dimension=1, tiled=True).reshape(token_count, -1)
    mine = lax.psum_scatter(mine, "fsdp", scatter_dimension=0, tiled=True)
    q_cols = w_query.shape[1] // tp_count
    attended = attend(
        mine[:, :q_cols], mine[:, q_cols:], lengths, key_cache, value_cache, step_count
    )
    everything = lax.all_gather(attended, "fsdp", axis=0, tiled=True)
    everything = lax.all_gather(everything, "tp", axis=1, tiled=True)
    features = contract_last(everything, w_out).astype(jnp.bfloat16)
    rows = lax.all_to_all(features, "fsdp", split_axis=0, concat_axis=1, tiled=True)
    near = fsdp_count // tp_count
    rows = rows.reshape(row_dev * step_count, tp_count, near, 1, depth)
    rows = lax.all_to_all(rows, "tp", split_axis=1, concat_axis=3, tiled=True)
    return rows.reshape(row_dev, step_count, -1)


def solution(mesh):
    return jax.shard_map(
        on_device,
        mesh=mesh,
        in_specs=(
            P(),
            P("fsdp"),
            P("tp", "fsdp"),
            P(),
            P(("fsdp", "tp"), None),
            P(("fsdp", "tp"), None),
            P(("fsdp", "tp"), None),
            P("fsdp", None, "tp"),
            P("fsdp", None, "tp"),
        ),
        out_specs=P("fsdp", None, "tp"),
        check_vma=False,
    )
```

```python
import functools
import math

import jax
import jax.numpy as jnp
from jax import lax
from jax.experimental import pallas as pl
from jax.experimental.pallas import tpu as pltpu
from jax.sharding import PartitionSpec as P

HD = 128


EPS_NORM = 1e-06
ROPE_BASE = 1000000.0


def rotate(vectors, positions):
    midpoint = vectors.shape[-1] // 2
    frequency = ROPE_BASE ** (-2.0 * jnp.arange(midpoint, dtype=jnp.float32) / vectors.shape[-1])
    angles = positions.astype(jnp.float32)[..., None, None] * frequency
    cosine = jnp.cos(angles)
    sine_part = jnp.sin(angles)
    leading = vectors[..., :midpoint]
    trailing = vectors[..., midpoint:]
    return jnp.concatenate(
        [leading * cosine - trailing * sine_part, trailing * cosine + leading * sine_part], -1
    )


def contract_last(left, right):
    return lax.dot_general(
        left, right, (((1,), (1,)), ((), ())), preferred_element_type=jnp.float32
    )


def attend(proj_q, proj_kv, lengths, key_cache, value_cache, step_count):
    row_dev = lengths.shape[0]
    context = key_cache.shape[1]
    positions = (lengths[:, None] + jnp.arange(step_count, dtype=jnp.int32)[None, :]).reshape(-1)
    queries = rotate(proj_q.reshape(row_dev * step_count, -1, HD), positions).astype(jnp.bfloat16)
    paired = proj_kv.reshape(row_dev * step_count, -1, 2, HD)
    new_keys = rotate(paired[:, :, 0, :], positions).astype(jnp.bfloat16)
    new_values = paired[:, :, 1, :].astype(jnp.bfloat16)
    kv_heads = key_cache.shape[2] // HD
    group_size = queries.shape[1] // kv_heads
    grouped = queries.reshape(row_dev, step_count, kv_heads, group_size, HD)
    old_keys = key_cache.reshape(row_dev, context, kv_heads, HD)
    old_values = value_cache.reshape(row_dev, context, kv_heads, HD)
    fresh_keys = new_keys.reshape(row_dev, step_count, kv_heads, HD)
    fresh_values = new_values.reshape(row_dev, step_count, kv_heads, HD)
    score_scale = 1.0 / math.sqrt(HD)
    old_scores = (
        jnp.einsum("rsghd,rjgd->rsghj", grouped, old_keys, preferred_element_type=jnp.float32)
        * score_scale
    )
    new_scores = (
        jnp.einsum("rsghd,rtgd->rsght", grouped, fresh_keys, preferred_element_type=jnp.float32)
        * score_scale
    )
    old_seen = (jnp.arange(context, dtype=jnp.int32)[None, :] < lengths[:, None])[
        :, None, None, None, :
    ]
    step_ids = jnp.arange(step_count, dtype=jnp.int32)
    new_seen = (step_ids[None, :] <= step_ids[:, None])[None, :, None, None, :]
    largest = jnp.maximum(
        jnp.max(jnp.where(old_seen, old_scores, -jnp.inf), -1, keepdims=True),
        jnp.max(jnp.where(new_seen, new_scores, -jnp.inf), -1, keepdims=True),
    )
    old_weights = jnp.where(old_seen, jnp.exp(old_scores - largest), 0.0)
    new_weights = jnp.where(new_seen, jnp.exp(new_scores - largest), 0.0)
    totals = jnp.sum(old_weights, -1, keepdims=True) + jnp.sum(new_weights, -1, keepdims=True)
    old_probs = (old_weights / totals).astype(jnp.bfloat16)
    new_probs = (new_weights / totals).astype(jnp.bfloat16)
    blended = jnp.einsum(
        "rsghj,rjgd->rsghd", old_probs, old_values, preferred_element_type=jnp.float32
    )
    blended = blended + jnp.einsum(
        "rsght,rtgd->rsghd", new_probs, fresh_values, preferred_element_type=jnp.float32
    )
    return blended.astype(jnp.bfloat16).reshape(row_dev * step_count, -1)


MESH = pl.DeviceIdType.MESH
VMEM_LIMIT = 48 * 1024 * 1024


def remote(src, dst, send_sem, recv_sem, device):
    return pltpu.make_async_remote_copy(
        src_ref=src,
        dst_ref=dst,
        send_sem=send_sem,
        recv_sem=recv_sem,
        device_id=device,
        device_id_type=MESH,
    )


def greet_all(me, count, tp_count):
    barrier = pltpu.get_barrier_semaphore()

    def greet(step, carry):
        other = lax.rem(me + step, count)
        pl.semaphore_signal(
            barrier, inc=1, device_id=(other // tp_count, lax.rem(other, tp_count)), device_id_type=MESH
        )
        return carry

    lax.fori_loop(1, count, greet, 0)
    pl.semaphore_wait(barrier, count - 1)


def project_kernel(
    fsdp_count, tp_count, picked, squares, gain, w_query, w_keyval, mine,
    wq_buf, wkv_buf, x_buf, sq_buf, away, kept, from_core, plane_out, from_plane, line_out, from_line,
    w_sem, x_send, x_recv, sq_send, sq_recv, core_send, core_recv, plane_send, plane_recv,
    line_send, line_recv,
):
    f = lax.axis_index("fsdp")
    t = lax.axis_index("tp")
    count = fsdp_count * tp_count
    me = f * tp_count + t
    fz, fy = f // 2, lax.rem(f, 2)
    xi, core = t // 2, lax.rem(t, 2)
    lines = fsdp_count // 2
    query_copy = pltpu.make_async_copy(w_query, wq_buf, w_sem.at[0])
    keyval_copy = pltpu.make_async_copy(w_keyval, wkv_buf, w_sem.at[1])
    query_copy.start()
    keyval_copy.start()
    greet_all(me, count, tp_count)

    def x_copy(step):
        other = lax.rem(t + step, tp_count)
        return remote(
            picked.at[other], x_buf.at[step - 1], x_send.at[step - 1], x_recv.at[step - 1], (f, other)
        )

    def sq_copy(step):
        other = lax.rem(me + step, count)
        return remote(
            squares, sq_buf.at[step - 1], sq_send.at[step - 1], sq_recv.at[step - 1],
            (other // tp_count, lax.rem(other, tp_count)),
        )

    for step in range(1, tp_count):
        x_copy(step).start()

    def send_sq(step, carry):
        sq_copy(step).start()
        return carry

    lax.fori_loop(1, count, send_sq, 0)
    inputs = picked[t].astype(jnp.float32)
    for step in range(1, tp_count):
        x_copy(step).wait_recv()
        inputs = inputs + x_buf[step - 1].astype(jnp.float32)

    def take_sq(step, total):
        sq_copy(step).wait_recv()
        return total + sq_buf[step - 1]

    total = lax.fori_loop(1, count, take_sq, squares[...])
    tokens, depth = inputs.shape
    column = jnp.transpose(jnp.broadcast_to(total[:1], (128, tokens)))[:, :1]
    scale_rows = lax.rsqrt(column / (depth * count) + EPS_NORM)
    normed = (inputs * scale_rows * gain[...]).astype(jnp.bfloat16)
    query_copy.wait()
    keyval_copy.wait()
    q_cols = wq_buf.shape[1] // tp_count
    kv_cols = wkv_buf.shape[1] // tp_count

    def project(head, store):
        for lo in range(0, q_cols, 512):
            columns = pl.ds(pl.multiple_of(head * q_cols + lo, 128), min(512, q_cols - lo))
            store(lo, jnp.dot(normed, wq_buf[:, columns], preferred_element_type=jnp.float32))
        columns = pl.ds(pl.multiple_of(head * kv_cols, 128), kv_cols)
        store(q_cols, jnp.dot(normed, wkv_buf[:, columns], preferred_element_type=jnp.float32))

    def core_copy(side):
        return remote(
            away.at[side], from_core.at[side], core_send.at[side], core_recv.at[side], (f, xi * 2 + 1 - core)
        )

    order = (lax.rem(xi + 1, 2), xi)
    for place in range(2):
        def store(lo, value, place=place):
            away[place, :, lo : lo + value.shape[1]] = value.astype(jnp.bfloat16)

        project(order[place] * 2 + 1 - core, store)

    for place in range(2):
        core_copy(place).start()
    for place in range(2):
        def store(lo, value, place=place):
            kept[place, :, lo : lo + value.shape[1]] = value

        project(order[place] * 2 + core, store)
    half = tokens // 2

    def plane_copy(dx, dy):
        slot = dx * 2 + dy - 1
        return remote(
            plane_out.at[slot], from_plane.at[slot], plane_send.at[slot], plane_recv.at[slot],
            (fz * 2 + lax.rem(fy + dy, 2), lax.rem(xi + dx, 2) * 2 + core),
        )

    core_copy(0).wait_recv()
    for dy in (1, 0):
        rows = pl.ds(pl.multiple_of(lax.rem(fy + dy, 2) * half, 16), half)
        plane_out[2 + dy - 1] = (
            kept[0, rows, :] + from_core[0, rows, :].astype(jnp.float32)
        ).astype(jnp.bfloat16)
        plane_copy(1, dy).start()
    core_copy(1).wait_recv()
    rows = pl.ds(pl.multiple_of(lax.rem(fy + 1, 2) * half, 16), half)
    plane_out[0] = (kept[1, rows, :] + from_core[1, rows, :].astype(jnp.float32)).astype(jnp.bfloat16)
    plane_copy(0, 1).start()
    rows = pl.ds(pl.multiple_of(fy * half, 16), half)
    own = kept[1, rows, :] + from_core[1, rows, :].astype(jnp.float32)
    plane_copy(0, 1).wait_recv()
    own = own + from_plane[0].astype(jnp.float32)
    plane_copy(1, 0).wait_recv()
    own = own + from_plane[1].astype(jnp.float32)
    plane_copy(1, 1).wait_recv()
    own = own + from_plane[2].astype(jnp.float32)
    block = half // lines
    kept[0, :half, :] = own
    line_out[...] = own.astype(jnp.bfloat16).reshape(line_out.shape)

    def line_copy(step):
        other = lax.rem(fz + step, lines)
        return remote(
            line_out.at[other], from_line.at[step - 1], line_send.at[step - 1], line_recv.at[step - 1],
            (other * 2 + fy, t),
        )

    for step in range(1, lines):
        line_copy(step).start()
    result = kept[0, pl.ds(pl.multiple_of(fz * block, 16), block), :]
    for step in range(1, lines):
        line_copy(step).wait_recv()
        result = result + from_line[step - 1].astype(jnp.float32)
    mine[...] = result
    for step in range(1, tp_count):
        x_copy(step).wait_send()

    def done_sq(step, carry):
        sq_copy(step).wait_send()
        return carry

    lax.fori_loop(1, count, done_sq, 0)
    for place in range(2):
        core_copy(place).wait_send()
    plane_copy(0, 1).wait_send()
    plane_copy(1, 0).wait_send()
    plane_copy(1, 1).wait_send()
    for step in range(1, lines):
        line_copy(step).wait_send()


def project(fsdp_count, tp_count, picked, squares, gain, w_query, w_keyval):
    _, tokens, depth = picked.shape
    count = fsdp_count * tp_count
    lines = fsdp_count // 2
    cols = (w_query.shape[1] + w_keyval.shape[1]) // tp_count
    half = tokens // 2
    dma = pltpu.SemaphoreType.DMA
    bf16, f32 = jnp.bfloat16, jnp.float32
    vmem = pl.BlockSpec(memory_space=pltpu.VMEM)
    hbm = pl.BlockSpec(memory_space=pl.ANY)
    return pl.pallas_call(
        functools.partial(project_kernel, fsdp_count, tp_count),
        out_shape=jax.ShapeDtypeStruct((tokens // fsdp_count, cols), f32),
        in_specs=[vmem, vmem, vmem, hbm, hbm],
        out_specs=vmem,
        scratch_shapes=[
            pltpu.VMEM(w_query.shape, bf16),
            pltpu.VMEM(w_keyval.shape, bf16),
            pltpu.VMEM((tp_count - 1, tokens, depth), bf16),
            pltpu.VMEM((count - 1,) + squares.shape, f32),
            pltpu.VMEM((2, tokens, cols), bf16),
            pltpu.VMEM((2, tokens, cols), f32),
            pltpu.VMEM((2, tokens, cols), bf16),
            pltpu.VMEM((3, half, cols), bf16),
            pltpu.VMEM((3, half, cols), bf16),
            pltpu.VMEM((lines, half // lines, cols), bf16),
            pltpu.VMEM((lines - 1, half // lines, cols), bf16),
            dma((2,)),
            dma((tp_count - 1,)), dma((tp_count - 1,)),
            dma((count - 1,)), dma((count - 1,)),
            dma((2,)), dma((2,)),
            dma((3,)), dma((3,)),
            dma((lines - 1,)), dma((lines - 1,)),
        ],
        compiler_params=pltpu.CompilerParams(
            collective_id=0, has_side_effects=True, vmem_limit_bytes=VMEM_LIMIT
        ),
        name="project",
    )(picked, squares, gain, w_query, w_keyval)


def output_kernel(
    fsdp_count, tp_count, attended, w_out, got,
    w_buf, parts, sums, blocks, gathered,
    w_sem, line_send, line_recv, plane_send, plane_recv, core_send, core_recv, out_send, out_recv,
):
    f = lax.axis_index("fsdp")
    t = lax.axis_index("tp")
    count = fsdp_count * tp_count
    fz, fy = f // 2, lax.rem(f, 2)
    xi, core = t // 2, lax.rem(t, 2)
    lines = fsdp_count // 2
    near = fsdp_count // tp_count
    weight_copy = pltpu.make_async_copy(w_out, w_buf, w_sem)
    weight_copy.start()
    parts[core, xi, fy, fz] = attended[...]
    greet_all(f * tp_count + t, count, tp_count)

    def line_copy(step, source):
        other = lax.rem(fz + step, lines)
        spot = parts.at[core, xi, fy, source]
        return remote(spot, spot, line_send.at[step - 1], line_recv.at[step - 1], (other * 2 + fy, t))

    def plane_copy(dx, dy, back):
        slot = dx * 2 + dy - 1
        other_x, other_y = lax.rem(xi + dx, 2), lax.rem(fy + dy, 2)
        spot = parts.at[core, other_x, other_y] if back else parts.at[core, xi, fy]
        return remote(
            spot, spot, plane_send.at[slot], plane_recv.at[slot], (fz * 2 + other_y, other_x * 2 + core)
        )

    def core_copy(dx, dy, back):
        slot = dx * 2 + dy
        side = 1 - core if back else core
        spot = parts.at[side, lax.rem(xi + dx, 2), lax.rem(fy + dy, 2)]
        return remote(spot, spot, core_send.at[slot], core_recv.at[slot], (f, xi * 2 + 1 - core))

    for step in range(1, lines):
        line_copy(step, fz).start()
    for step in range(1, lines):
        line_copy(step, lax.rem(fz - step + lines, lines)).wait_recv()
    peers = ((1, 1), (1, 0), (0, 1))
    for dx, dy in peers:
        plane_copy(dx, dy, False).start()
    core_copy(0, 0, False).start()
    for dx, dy in reversed(peers):
        plane_copy(dx, dy, True).wait_recv()
        core_copy(dx, dy, False).start()
    weight_copy.wait()
    tokens = sums.shape[0]
    cols = w_buf.shape[1] // tp_count

    def add(side, far, first):
        columns = pl.ds(pl.multiple_of((far * 2 + side) * cols, 128), cols)
        value = contract_last(parts[side, far].reshape(tokens, cols), w_buf[:, columns])
        if first:
            sums[...] = value
        else:
            sums[...] += value

    add(core, xi, True)
    add(core, lax.rem(xi + 1, 2), False)
    for dx, dy in ((0, 0),) + tuple(reversed(peers)):
        core_copy(dx, dy, True).wait_recv()
    add(1 - core, xi, False)
    add(1 - core, lax.rem(xi + 1, 2), False)
    blocks[...] = sums[...].astype(jnp.bfloat16).reshape(blocks.shape)
    target = f // near
    place = lax.rem(f, near) * tp_count + t

    def out_copy(step):
        other = lax.rem(f + step, fsdp_count)
        return remote(
            blocks.at[lax.rem(other, 2) * lines + other // 2], gathered.at[place],
            out_send.at[step], out_recv.at[place], (other, target),
        )

    for step in range(1, fsdp_count):
        out_copy(step).start()

    @pl.when(target != t)
    def _():
        out_copy(0).start()

    @pl.when(target == t)
    def _():
        gathered[place] = blocks[fy * lines + fz]

    def source(slot):
        return t * near + slot // tp_count, slot % tp_count

    for slot in range(near * tp_count):
        sender_f, sender_t = source(slot)

        @pl.when(jnp.logical_or(sender_f != f, sender_t != t))
        def _(slot=slot, sender_f=sender_f, sender_t=sender_t):
            remote(
                blocks.at[0], gathered.at[slot], out_send.at[0], out_recv.at[slot], (sender_f, sender_t)
            ).wait_recv()

    got[...] = gathered[...]
    for step in range(1, lines):
        line_copy(step, fz).wait_send()
    for dx, dy in peers:
        plane_copy(dx, dy, False).wait_send()
    for dx, dy in ((0, 0),) + peers:
        core_copy(dx, dy, False).wait_send()
    for step in range(1, fsdp_count):
        out_copy(step).wait_send()

    @pl.when(target != t)
    def _():
        out_copy(0).wait_send()


def output(fsdp_count, tp_count, attended, w_out):
    row_tokens, cols = attended.shape
    depth = w_out.shape[0]
    lines = fsdp_count // 2
    slots = (fsdp_count // tp_count) * tp_count
    dma = pltpu.SemaphoreType.DMA
    vmem = pl.BlockSpec(memory_space=pltpu.VMEM)
    return pl.pallas_call(
        functools.partial(output_kernel, fsdp_count, tp_count),
        out_shape=jax.ShapeDtypeStruct((slots, row_tokens, depth), jnp.bfloat16),
        in_specs=[vmem, pl.BlockSpec(memory_space=pl.ANY)],
        out_specs=vmem,
        scratch_shapes=[
            pltpu.VMEM(w_out.shape, jnp.bfloat16),
            pltpu.VMEM((2, 2, 2, lines, row_tokens, cols), jnp.bfloat16),
            pltpu.VMEM((fsdp_count * row_tokens, depth), jnp.float32),
            pltpu.VMEM((fsdp_count, row_tokens, depth), jnp.bfloat16),
            pltpu.VMEM((slots, row_tokens, depth), jnp.bfloat16),
            dma,
            dma((lines - 1,)), dma((lines - 1,)),
            dma((3,)), dma((3,)),
            dma((4,)), dma((4,)),
            dma((fsdp_count,)), dma((slots,)),
        ],
        compiler_params=pltpu.CompilerParams(
            collective_id=1, has_side_effects=True, vmem_limit_bytes=VMEM_LIMIT
        ),
        name="output",
    )(attended, w_out)


def on_device(
    token_ids, lengths, embedding, norm_gain, w_query, w_keyval, w_out, key_cache, value_cache
):
    tp_count = lax.axis_size("tp")
    fsdp_count = lax.axis_size("fsdp")
    tp_rank = lax.axis_index("tp")
    fsdp_rank = lax.axis_index("fsdp")
    step_count = token_ids.shape[1]
    row_dev = lengths.shape[0]
    vocab_part = embedding.shape[0]
    token_count = token_ids.size
    depth = w_query.shape[0]
    ordered = token_ids.reshape(fsdp_count // 2, 2, -1).transpose(1, 0, 2).reshape(-1)
    shifted = ordered - tp_rank * vocab_part
    inside = (shifted >= 0) & (shifted < vocab_part)
    picked = jnp.take(embedding, jnp.clip(shifted, 0, vocab_part - 1), axis=0)
    picked = jnp.where(inside[:, None], picked, jnp.zeros_like(picked))
    wide = picked.astype(jnp.float32)
    squares = jnp.broadcast_to(jnp.sum(wide * wide, -1)[None, :], (8, token_count))
    picked = picked.reshape(token_count, tp_count, depth).transpose(1, 0, 2)
    gain = lax.dynamic_slice(norm_gain, ((fsdp_rank * tp_count + tp_rank) * depth,), (depth,))
    mine = project(fsdp_count, tp_count, picked, squares, gain[None, :], w_query, w_keyval)
    q_cols = w_query.shape[1] // tp_count
    attended = attend(
        mine[:, :q_cols], mine[:, q_cols:], lengths, key_cache, value_cache, step_count
    )
    rows = output(fsdp_count, tp_count, attended, w_out)
    return rows.transpose(1, 0, 2).reshape(row_dev, step_count, -1)


def solution(mesh):
    return jax.shard_map(
        on_device,
        mesh=mesh,
        in_specs=(
            P(),
            P("fsdp"),
            P("tp", "fsdp"),
            P(),
            P(("fsdp", "tp"), None),
            P(("fsdp", "tp"), None),
            P(("fsdp", "tp"), None),
            P("fsdp", None, "tp"),
            P("fsdp", None, "tp"),
        ),
        out_specs=P("fsdp", None, "tp"),
        check_vma=False,
    )
```

```python
import functools
import math

import jax
import jax.numpy as jnp
from jax import lax
from jax.experimental import pallas as pl
from jax.experimental.pallas import tpu as pltpu
from jax.sharding import PartitionSpec as P

HD = 128


EPS_NORM = 1e-06
ROPE_BASE = 1000000.0


def contract_last(left, right):
    return lax.dot_general(
        left, right, (((1,), (1,)), ((), ())), preferred_element_type=jnp.float32
    )


MESH = pl.DeviceIdType.MESH
VMEM_LIMIT = 48 * 1024 * 1024


def remote(src, dst, send_sem, recv_sem, device):
    return pltpu.make_async_remote_copy(
        src_ref=src,
        dst_ref=dst,
        send_sem=send_sem,
        recv_sem=recv_sem,
        device_id=device,
        device_id_type=MESH,
    )


def greet_all(me, count, tp_count):
    barrier = pltpu.get_barrier_semaphore()

    def greet(step, carry):
        other = lax.rem(me + step, count)
        pl.semaphore_signal(
            barrier, inc=1, device_id=(other // tp_count, lax.rem(other, tp_count)), device_id_type=MESH
        )
        return carry

    lax.fori_loop(1, count, greet, 0)
    pl.semaphore_wait(barrier, count - 1)


def attend_rows(
    projected, q_cols, kv_cols, lengths, cosine, sine_part, keys, values, key_copies, value_copies, attended
):
    tokens = projected.shape[0]
    row_dev, context, _ = keys.shape
    steps = tokens // row_dev
    heads = q_cols // HD
    lanes = heads * steps
    score_scale = 1.0 / math.sqrt(HD)

    def turned(lo):
        vectors = projected[:, lo : lo + HD]
        swapped = pltpu.roll(vectors, HD // 2, 1)
        return (vectors * cosine[...] + swapped * sine_part[...]).astype(jnp.bfloat16)

    queries = jnp.concatenate([turned(h * HD) for h in range(heads)], 0)
    new_keys = turned(q_cols)
    new_values = projected[:, q_cols + HD : q_cols + 2 * HD].astype(jnp.bfloat16)
    total_rows = heads * tokens
    pick_row = lax.broadcasted_iota(jnp.int32, (lanes, total_rows), 0)
    pick_col = lax.broadcasted_iota(jnp.int32, (lanes, total_rows), 1)
    picked_col = pick_row // steps * tokens + pick_row % steps
    new_row = lax.broadcasted_iota(jnp.int32, (lanes, tokens), 0) % steps
    new_col = lax.broadcasted_iota(jnp.int32, (lanes, tokens), 1)
    slots = lax.broadcasted_iota(jnp.int32, (lanes, context), 1)
    outs = []
    for r in range(row_dev):
        choose = jnp.where(pick_col == picked_col + r * steps, 1.0, 0.0).astype(jnp.bfloat16)
        query = jnp.dot(choose, queries, preferred_element_type=jnp.float32).astype(jnp.bfloat16)
        key_copies[r].wait()
        old_scores = contract_last(query, keys[r]) * score_scale
        new_scores = contract_last(query, new_keys) * score_scale
        step_of = new_col - r * steps
        old_scores = jnp.where(slots < lengths[r], old_scores, -jnp.inf)
        new_scores = jnp.where((step_of >= 0) & (step_of <= new_row), new_scores, -jnp.inf)
        largest = jnp.maximum(
            jnp.max(old_scores, -1, keepdims=True), jnp.max(new_scores, -1, keepdims=True)
        )
        old_weights = jnp.exp(old_scores - largest)
        new_weights = jnp.exp(new_scores - largest)
        share = 1.0 / (
            jnp.sum(old_weights, -1, keepdims=True) + jnp.sum(new_weights, -1, keepdims=True)
        )
        value_copies[r].wait()
        blended = jnp.dot(
            (old_weights * share).astype(jnp.bfloat16), values[r], preferred_element_type=jnp.float32
        ) + jnp.dot(
            (new_weights * share).astype(jnp.bfloat16), new_values, preferred_element_type=jnp.float32
        )
        outs.append(blended.astype(jnp.bfloat16))
    stacked = jnp.concatenate(outs, 0)
    back_row = lax.broadcasted_iota(jnp.int32, (total_rows, total_rows), 0)
    back_col = lax.broadcasted_iota(jnp.int32, (total_rows, total_rows), 1)
    token = back_row % tokens
    wanted = token // steps * lanes + back_row // tokens * steps + token % steps
    choose = jnp.where(back_col == wanted, 1.0, 0.0).astype(jnp.bfloat16)
    ordered = jnp.dot(choose, stacked, preferred_element_type=jnp.float32).astype(jnp.bfloat16)
    for h in range(heads):
        attended[:, h * HD : (h + 1) * HD] = ordered[h * tokens : (h + 1) * tokens]


def block_kernel(
    fsdp_count, tp_count, lengths, picked, squares, gain, cosine, sine_part, w_query, w_keyval, w_out, key_cache,
    value_cache, got,
    wq_buf, wkv_buf, x_buf, sq_buf, away, kept, from_core, plane_out, from_plane, line_out, from_line,
    w_buf, parts, sums, blocks, gathered, keys, values,
    w_sem, cache_sem, x_send, x_recv, sq_send, sq_recv, core_send, core_recv, plane_send, plane_recv,
    line_send, line_recv, aline_send, aline_recv, aplane_send, aplane_recv, acore_send, acore_recv,
    out_send, out_recv,
):
    f = lax.axis_index("fsdp")
    t = lax.axis_index("tp")
    count = fsdp_count * tp_count
    me = f * tp_count + t
    fz, fy = f // 2, lax.rem(f, 2)
    xi, core = t // 2, lax.rem(t, 2)
    lines = fsdp_count // 2
    query_copy = pltpu.make_async_copy(w_query, wq_buf, w_sem.at[0])
    keyval_copy = pltpu.make_async_copy(w_keyval, wkv_buf, w_sem.at[1])
    query_copy.start()
    keyval_copy.start()
    key_copies = [
        pltpu.make_async_copy(key_cache.at[r], keys.at[r], cache_sem.at[0, r])
        for r in range(keys.shape[0])
    ]
    value_copies = [
        pltpu.make_async_copy(value_cache.at[r], values.at[r], cache_sem.at[1, r])
        for r in range(keys.shape[0])
    ]
    weight_copy = pltpu.make_async_copy(w_out, w_buf, w_sem.at[2])
    for copy in key_copies + value_copies + [weight_copy]:
        copy.start()
    greet_all(me, count, tp_count)

    def x_copy(step):
        other = lax.rem(t + step, tp_count)
        return remote(
            picked.at[other], x_buf.at[step - 1], x_send.at[step - 1], x_recv.at[step - 1], (f, other)
        )

    def sq_copy(step):
        other = lax.rem(me + step, count)
        return remote(
            squares, sq_buf.at[step - 1], sq_send.at[step - 1], sq_recv.at[step - 1],
            (other // tp_count, lax.rem(other, tp_count)),
        )

    for step in range(1, tp_count):
        x_copy(step).start()

    def send_sq(step, carry):
        sq_copy(step).start()
        return carry

    lax.fori_loop(1, count, send_sq, 0)
    inputs = picked[t].astype(jnp.float32)
    for step in range(1, tp_count):
        x_copy(step).wait_recv()
        inputs = inputs + x_buf[step - 1].astype(jnp.float32)

    def take_sq(step, total):
        sq_copy(step).wait_recv()
        return total + sq_buf[step - 1]

    total = lax.fori_loop(1, count, take_sq, squares[...])
    tokens, depth = inputs.shape
    column = jnp.transpose(jnp.broadcast_to(total[:1], (128, tokens)))[:, :1]
    scale_rows = lax.rsqrt(column / (depth * count) + EPS_NORM)
    normed = (inputs * scale_rows * gain[...]).astype(jnp.bfloat16)
    query_copy.wait()
    keyval_copy.wait()
    q_cols = wq_buf.shape[1] // tp_count
    kv_cols = wkv_buf.shape[1] // tp_count

    def project(head, store):
        for lo in range(0, q_cols, 512):
            columns = pl.ds(pl.multiple_of(head * q_cols + lo, 128), min(512, q_cols - lo))
            store(lo, jnp.dot(normed, wq_buf[:, columns], preferred_element_type=jnp.float32))
        columns = pl.ds(pl.multiple_of(head * kv_cols, 128), kv_cols)
        store(q_cols, jnp.dot(normed, wkv_buf[:, columns], preferred_element_type=jnp.float32))

    def core_copy(side):
        return remote(
            away.at[side], from_core.at[side], core_send.at[side], core_recv.at[side], (f, xi * 2 + 1 - core)
        )

    order = (lax.rem(xi + 1, 2), xi)
    for place in range(2):
        def store(lo, value, place=place):
            away[place, :, lo : lo + value.shape[1]] = value.astype(jnp.bfloat16)

        project(order[place] * 2 + 1 - core, store)
        core_copy(place).start()

    for place in range(2):
        def store(lo, value, place=place):
            kept[place, :, lo : lo + value.shape[1]] = value

        project(order[place] * 2 + core, store)
    half = tokens // 2

    def plane_copy(dx, dy):
        slot = dx * 2 + dy - 1
        return remote(
            plane_out.at[slot], from_plane.at[slot], plane_send.at[slot], plane_recv.at[slot],
            (fz * 2 + lax.rem(fy + dy, 2), lax.rem(xi + dx, 2) * 2 + core),
        )

    core_copy(0).wait_recv()
    for dy in (1, 0):
        rows = pl.ds(pl.multiple_of(lax.rem(fy + dy, 2) * half, 16), half)
        plane_out[2 + dy - 1] = (
            kept[0, rows, :] + from_core[0, rows, :].astype(jnp.float32)
        ).astype(jnp.bfloat16)
        plane_copy(1, dy).start()
    core_copy(1).wait_recv()
    rows = pl.ds(pl.multiple_of(lax.rem(fy + 1, 2) * half, 16), half)
    plane_out[0] = (kept[1, rows, :] + from_core[1, rows, :].astype(jnp.float32)).astype(jnp.bfloat16)
    plane_copy(0, 1).start()
    rows = pl.ds(pl.multiple_of(fy * half, 16), half)
    own = kept[1, rows, :] + from_core[1, rows, :].astype(jnp.float32)
    plane_copy(0, 1).wait_recv()
    own = own + from_plane[0].astype(jnp.float32)
    plane_copy(1, 0).wait_recv()
    own = own + from_plane[1].astype(jnp.float32)
    plane_copy(1, 1).wait_recv()
    own = own + from_plane[2].astype(jnp.float32)
    block = half // lines
    kept[0, :half, :] = own
    line_out[...] = own.astype(jnp.bfloat16).reshape(line_out.shape)

    def line_copy(step):
        other = lax.rem(fz + step, lines)
        return remote(
            line_out.at[other], from_line.at[step - 1], line_send.at[step - 1], line_recv.at[step - 1],
            (other * 2 + fy, t),
        )

    for step in range(1, lines):
        line_copy(step).start()
    result = kept[0, pl.ds(pl.multiple_of(fz * block, 16), block), :]
    for step in range(1, lines):
        line_copy(step).wait_recv()
        result = result + from_line[step - 1].astype(jnp.float32)
    attend_rows(
        result, q_cols, kv_cols, lengths, cosine, sine_part, keys, values, key_copies, value_copies,
        parts.at[core, xi, fy, fz],
    )
    near = fsdp_count // tp_count
    def aline_copy(step, source):
        other = lax.rem(fz + step, lines)
        spot = parts.at[core, xi, fy, source]
        return remote(spot, spot, aline_send.at[step - 1], aline_recv.at[step - 1], (other * 2 + fy, t))

    def aplane_copy(dx, dy, back):
        slot = dx * 2 + dy - 1
        other_x, other_y = lax.rem(xi + dx, 2), lax.rem(fy + dy, 2)
        spot = parts.at[core, other_x, other_y] if back else parts.at[core, xi, fy]
        return remote(
            spot, spot, aplane_send.at[slot], aplane_recv.at[slot], (fz * 2 + other_y, other_x * 2 + core)
        )

    def acore_copy(dx, dy, back):
        slot = dx * 2 + dy
        side = 1 - core if back else core
        spot = parts.at[side, lax.rem(xi + dx, 2), lax.rem(fy + dy, 2)]
        return remote(spot, spot, acore_send.at[slot], acore_recv.at[slot], (f, xi * 2 + 1 - core))

    for step in range(1, lines):
        aline_copy(step, fz).start()
    for step in range(1, lines):
        aline_copy(step, lax.rem(fz - step + lines, lines)).wait_recv()
    peers = ((1, 1), (1, 0), (0, 1))
    for dx, dy in peers:
        aplane_copy(dx, dy, False).start()
    acore_copy(0, 0, False).start()
    for dx, dy in reversed(peers):
        aplane_copy(dx, dy, True).wait_recv()
        acore_copy(dx, dy, False).start()
    weight_copy.wait()
    cols = w_buf.shape[1] // tp_count

    def add(side, far, first):
        columns = pl.ds(pl.multiple_of((far * 2 + side) * cols, 128), cols)
        value = contract_last(parts[side, far].reshape(tokens, cols), w_buf[:, columns])
        if first:
            sums[...] = value
        else:
            sums[...] += value

    add(core, xi, True)
    add(core, lax.rem(xi + 1, 2), False)
    for dx, dy in ((0, 0),) + tuple(reversed(peers)):
        acore_copy(dx, dy, True).wait_recv()
    add(1 - core, xi, False)
    add(1 - core, lax.rem(xi + 1, 2), False)
    blocks[...] = sums[...].astype(jnp.bfloat16).reshape(blocks.shape)
    target = f // near
    place = lax.rem(f, near) * tp_count + t

    def out_copy(step):
        other = lax.rem(f + step, fsdp_count)
        return remote(
            blocks.at[lax.rem(other, 2) * lines + other // 2], gathered.at[place],
            out_send.at[step], out_recv.at[place], (other, target),
        )

    for step in range(1, fsdp_count):
        out_copy(step).start()

    @pl.when(target != t)
    def _():
        out_copy(0).start()

    @pl.when(target == t)
    def _():
        gathered[place] = blocks[fy * lines + fz]

    def source(slot):
        return t * near + slot // tp_count, slot % tp_count

    for slot in range(near * tp_count):
        sender_f, sender_t = source(slot)

        @pl.when(jnp.logical_or(sender_f != f, sender_t != t))
        def _(slot=slot, sender_f=sender_f, sender_t=sender_t):
            remote(
                blocks.at[0], gathered.at[slot], out_send.at[0], out_recv.at[slot], (sender_f, sender_t)
            ).wait_recv()

    got[...] = gathered[...]
    for step in range(1, lines):
        aline_copy(step, fz).wait_send()
    for dx, dy in peers:
        aplane_copy(dx, dy, False).wait_send()
    for dx, dy in ((0, 0),) + peers:
        acore_copy(dx, dy, False).wait_send()
    for step in range(1, fsdp_count):
        out_copy(step).wait_send()

    @pl.when(target != t)
    def _():
        out_copy(0).wait_send()
    for step in range(1, tp_count):
        x_copy(step).wait_send()

    def done_sq(step, carry):
        sq_copy(step).wait_send()
        return carry

    lax.fori_loop(1, count, done_sq, 0)
    for place in range(2):
        core_copy(place).wait_send()
    plane_copy(0, 1).wait_send()
    plane_copy(1, 0).wait_send()
    plane_copy(1, 1).wait_send()
    for step in range(1, lines):
        line_copy(step).wait_send()


def block(
    fsdp_count, tp_count, lengths, picked, squares, gain, cosine, sine_part, w_query, w_keyval, w_out,
    key_cache, value_cache
):
    _, tokens, depth = picked.shape
    count = fsdp_count * tp_count
    lines = fsdp_count // 2
    cols = (w_query.shape[1] + w_keyval.shape[1]) // tp_count
    half = tokens // 2
    row_tokens = tokens // fsdp_count
    out_cols = w_out.shape[1] // tp_count
    slots = fsdp_count // tp_count * tp_count
    dma = pltpu.SemaphoreType.DMA
    bf16, f32 = jnp.bfloat16, jnp.float32
    vmem = pl.BlockSpec(memory_space=pltpu.VMEM)
    hbm = pl.BlockSpec(memory_space=pltpu.HBM)
    return pl.pallas_call(
        functools.partial(block_kernel, fsdp_count, tp_count),
        out_shape=jax.ShapeDtypeStruct((slots, row_tokens, depth), bf16),
        in_specs=[pl.BlockSpec(memory_space=pltpu.SMEM)] + [vmem] * 5 + [hbm] * 5,
        out_specs=vmem,
        scratch_shapes=[
            pltpu.VMEM(w_query.shape, bf16),
            pltpu.VMEM(w_keyval.shape, bf16),
            pltpu.VMEM((tp_count - 1, tokens, depth), bf16),
            pltpu.VMEM((count - 1,) + squares.shape, f32),
            pltpu.VMEM((2, tokens, cols), bf16),
            pltpu.VMEM((2, tokens, cols), f32),
            pltpu.VMEM((2, tokens, cols), bf16),
            pltpu.VMEM((3, half, cols), bf16),
            pltpu.VMEM((3, half, cols), bf16),
            pltpu.VMEM((lines, half // lines, cols), bf16),
            pltpu.VMEM((lines - 1, half // lines, cols), bf16),
            pltpu.VMEM(w_out.shape, bf16),
            pltpu.VMEM((2, 2, 2, lines, row_tokens, out_cols), bf16),
            pltpu.VMEM((tokens, depth), f32),
            pltpu.VMEM((fsdp_count, row_tokens, depth), bf16),
            pltpu.VMEM((slots, row_tokens, depth), bf16),
            pltpu.VMEM(key_cache.shape, bf16),
            pltpu.VMEM(value_cache.shape, bf16),
            dma((3,)), dma((2, key_cache.shape[0])),
            dma((tp_count - 1,)), dma((tp_count - 1,)),
            dma((count - 1,)), dma((count - 1,)),
            dma((2,)), dma((2,)),
            dma((3,)), dma((3,)),
            dma((lines - 1,)), dma((lines - 1,)),
            dma((lines - 1,)), dma((lines - 1,)),
            dma((3,)), dma((3,)),
            dma((4,)), dma((4,)),
            dma((fsdp_count,)), dma((slots,)),
        ],
        compiler_params=pltpu.CompilerParams(
            collective_id=0, has_side_effects=True, vmem_limit_bytes=VMEM_LIMIT
        ),
        name="block",
    )(
        lengths, picked, squares, gain, cosine, sine_part, w_query, w_keyval, w_out, key_cache, value_cache
    )


def on_device(
    token_ids, lengths, embedding, norm_gain, w_query, w_keyval, w_out, key_cache, value_cache
):
    tp_count = lax.axis_size("tp")
    fsdp_count = lax.axis_size("fsdp")
    tp_rank = lax.axis_index("tp")
    fsdp_rank = lax.axis_index("fsdp")
    step_count = token_ids.shape[1]
    row_dev = lengths.shape[0]
    vocab_part = embedding.shape[0]
    token_count = token_ids.size
    depth = w_query.shape[0]
    ordered = token_ids.reshape(fsdp_count // 2, 2, -1).transpose(1, 0, 2).reshape(-1)
    shifted = ordered - tp_rank * vocab_part
    picked = embedding.at[shifted].get(mode="fill", fill_value=0, wrap_negative_indices=False)
    wide = picked.astype(jnp.float32)
    squares = jnp.broadcast_to(jnp.sum(wide * wide, -1)[None, :], (8, token_count))
    picked = picked.reshape(token_count, tp_count, depth).transpose(1, 0, 2)
    gain = lax.dynamic_slice(norm_gain, ((fsdp_rank * tp_count + tp_rank) * depth,), (depth,))
    positions = (lengths[:, None] + jnp.arange(step_count, dtype=jnp.int32)[None, :]).reshape(-1)
    midpoint = HD // 2
    frequency = ROPE_BASE ** (-2.0 * jnp.arange(midpoint, dtype=jnp.float32) / HD)
    angles = positions.astype(jnp.float32)[:, None] * frequency
    cosine = jnp.cos(angles)
    sine_part = jnp.sin(angles)
    rows = block(
        fsdp_count, tp_count, lengths, picked, squares, gain[None, :],
        jnp.concatenate([cosine, cosine], -1), jnp.concatenate([-sine_part, sine_part], -1),
        w_query, w_keyval, w_out, key_cache, value_cache,
    )
    return rows.transpose(1, 0, 2).reshape(row_dev, step_count, -1)


def solution(mesh):
    return jax.shard_map(
        on_device,
        mesh=mesh,
        in_specs=(
            P(),
            P("fsdp"),
            P("tp", "fsdp"),
            P(),
            P(("fsdp", "tp"), None),
            P(("fsdp", "tp"), None),
            P(("fsdp", "tp"), None),
            P("fsdp", None, "tp"),
            P("fsdp", None, "tp"),
        ),
        out_specs=P("fsdp", None, "tp"),
        check_vma=False,
    )
```

```python
import functools
import math

import jax
import jax.numpy as jnp
from jax import lax
from jax.experimental import pallas as pl
from jax.experimental.pallas import tpu as pltpu
from jax.sharding import PartitionSpec as P

HD = 128


EPS_NORM = 1e-06
ROPE_BASE = 1000000.0


def contract_last(left, right):
    return lax.dot_general(
        left, right, (((1,), (1,)), ((), ())), preferred_element_type=jnp.float32
    )


MESH = pl.DeviceIdType.MESH
VMEM_LIMIT = 48 * 1024 * 1024


def remote(src, dst, send_sem, recv_sem, device):
    return pltpu.make_async_remote_copy(
        src_ref=src,
        dst_ref=dst,
        send_sem=send_sem,
        recv_sem=recv_sem,
        device_id=device,
        device_id_type=MESH,
    )


def greet_all(me, count, tp_count):
    barrier = pltpu.get_barrier_semaphore()

    def greet(step, carry):
        other = lax.rem(me + step, count)
        pl.semaphore_signal(
            barrier, inc=1, device_id=(other // tp_count, lax.rem(other, tp_count)), device_id_type=MESH
        )
        return carry

    lax.fori_loop(1, count, greet, 0)
    pl.semaphore_wait(barrier, count - 1)


def attend_rows(
    projected, q_cols, kv_cols, lengths, cosine, sine_part, keys, values, key_copies, value_copies, attended
):
    tokens = projected.shape[0]
    row_dev, context, _ = keys.shape
    steps = tokens // row_dev
    heads = q_cols // HD
    lanes = heads * steps
    score_scale = 1.0 / math.sqrt(HD)

    def turned(lo):
        vectors = projected[:, lo : lo + HD]
        swapped = pltpu.roll(vectors, HD // 2, 1)
        return (vectors * cosine[...] + swapped * sine_part[...]).astype(jnp.bfloat16)

    queries = jnp.concatenate([turned(h * HD) for h in range(heads)], 0)
    new_keys = turned(q_cols)
    new_values = projected[:, q_cols + HD : q_cols + 2 * HD].astype(jnp.bfloat16)
    total_rows = heads * tokens
    pick_row = lax.broadcasted_iota(jnp.int32, (lanes, total_rows), 0)
    pick_col = lax.broadcasted_iota(jnp.int32, (lanes, total_rows), 1)
    picked_col = pick_row // steps * tokens + pick_row % steps
    new_row = lax.broadcasted_iota(jnp.int32, (lanes, tokens), 0) % steps
    new_col = lax.broadcasted_iota(jnp.int32, (lanes, tokens), 1)
    slots = lax.broadcasted_iota(jnp.int32, (lanes, context), 1)
    outs = []
    for r in range(row_dev):
        choose = jnp.where(pick_col == picked_col + r * steps, 1.0, 0.0).astype(jnp.bfloat16)
        query = jnp.dot(choose, queries, preferred_element_type=jnp.float32).astype(jnp.bfloat16)
        key_copies[r].wait()
        old_scores = contract_last(query, keys[r]) * score_scale
        new_scores = contract_last(query, new_keys) * score_scale
        step_of = new_col - r * steps
        old_scores = jnp.where(slots < lengths[r], old_scores, -jnp.inf)
        new_scores = jnp.where((step_of >= 0) & (step_of <= new_row), new_scores, -jnp.inf)
        largest = jnp.maximum(
            jnp.max(old_scores, -1, keepdims=True), jnp.max(new_scores, -1, keepdims=True)
        )
        old_weights = jnp.exp(old_scores - largest)
        new_weights = jnp.exp(new_scores - largest)
        share = 1.0 / (
            jnp.sum(old_weights, -1, keepdims=True) + jnp.sum(new_weights, -1, keepdims=True)
        )
        value_copies[r].wait()
        blended = jnp.dot(
            (old_weights * share).astype(jnp.bfloat16), values[r], preferred_element_type=jnp.float32
        ) + jnp.dot(
            (new_weights * share).astype(jnp.bfloat16), new_values, preferred_element_type=jnp.float32
        )
        outs.append(blended.astype(jnp.bfloat16))
    stacked = jnp.concatenate(outs, 0)
    back_row = lax.broadcasted_iota(jnp.int32, (total_rows, total_rows), 0)
    back_col = lax.broadcasted_iota(jnp.int32, (total_rows, total_rows), 1)
    token = back_row % tokens
    wanted = token // steps * lanes + back_row // tokens * steps + token % steps
    choose = jnp.where(back_col == wanted, 1.0, 0.0).astype(jnp.bfloat16)
    ordered = jnp.dot(choose, stacked, preferred_element_type=jnp.float32).astype(jnp.bfloat16)
    for h in range(heads):
        attended[:, h * HD : (h + 1) * HD] = ordered[h * tokens : (h + 1) * tokens]


def block_kernel(
    fsdp_count, tp_count, lengths, picked, squares, gain, cosine, sine_part, w_query, w_keyval, w_out, key_cache,
    value_cache, got,
    wq_buf, wkv_buf, x_buf, sq_buf, away, kept, from_core, plane_out, from_plane, line_out, from_line,
    w_buf, parts, sums, blocks, gathered, keys, values,
    w_sem, cache_sem, x_send, x_recv, sq_send, sq_recv, core_send, core_recv, plane_send, plane_recv,
    line_send, line_recv, aline_send, aline_recv, aplane_send, aplane_recv, acore_send, acore_recv,
    out_send, out_recv,
):
    f = lax.axis_index("fsdp")
    t = lax.axis_index("tp")
    count = fsdp_count * tp_count
    me = f * tp_count + t
    fz, fy = f // 2, lax.rem(f, 2)
    xi, core = t // 2, lax.rem(t, 2)
    lines = fsdp_count // 2
    query_copy = pltpu.make_async_copy(w_query, wq_buf, w_sem.at[0])
    keyval_copy = pltpu.make_async_copy(w_keyval, wkv_buf, w_sem.at[1])
    query_copy.start()
    keyval_copy.start()
    key_copies = [
        pltpu.make_async_copy(key_cache.at[r], keys.at[r], cache_sem.at[0, r])
        for r in range(keys.shape[0])
    ]
    value_copies = [
        pltpu.make_async_copy(value_cache.at[r], values.at[r], cache_sem.at[1, r])
        for r in range(keys.shape[0])
    ]
    weight_copy = pltpu.make_async_copy(w_out, w_buf, w_sem.at[2])
    for copy in key_copies + value_copies + [weight_copy]:
        copy.start()
    greet_all(me, count, tp_count)

    def x_copy(step):
        other = lax.rem(t + step, tp_count)
        return remote(
            picked.at[other], x_buf.at[step - 1], x_send.at[step - 1], x_recv.at[step - 1], (f, other)
        )

    def sq_copy(step):
        other = lax.rem(me + step, count)
        return remote(
            squares, sq_buf.at[step - 1], sq_send.at[step - 1], sq_recv.at[step - 1],
            (other // tp_count, lax.rem(other, tp_count)),
        )

    for step in range(1, tp_count):
        x_copy(step).start()

    def send_sq(step, carry):
        sq_copy(step).start()
        return carry

    lax.fori_loop(1, count, send_sq, 0)
    inputs = picked[t].astype(jnp.float32)
    for step in range(1, tp_count):
        x_copy(step).wait_recv()
        inputs = inputs + x_buf[step - 1].astype(jnp.float32)

    def take_sq(step, total):
        sq_copy(step).wait_recv()
        return total + sq_buf[step - 1]

    total = lax.fori_loop(1, count, take_sq, squares[...])
    tokens, depth = inputs.shape
    column = jnp.transpose(jnp.broadcast_to(total[:1], (128, tokens)))[:, :1]
    scale_rows = lax.rsqrt(column / (depth * count) + EPS_NORM)
    normed = (inputs * scale_rows * gain[...]).astype(jnp.bfloat16)
    query_copy.wait()
    keyval_copy.wait()
    q_cols = wq_buf.shape[1] // tp_count
    kv_cols = wkv_buf.shape[1] // tp_count

    def project(head, store):
        for lo in range(0, q_cols, 512):
            columns = pl.ds(pl.multiple_of(head * q_cols + lo, 128), min(512, q_cols - lo))
            store(lo, jnp.dot(normed, wq_buf[:, columns], preferred_element_type=jnp.float32))
        columns = pl.ds(pl.multiple_of(head * kv_cols, 128), kv_cols)
        store(q_cols, jnp.dot(normed, wkv_buf[:, columns], preferred_element_type=jnp.float32))

    def core_copy(side):
        return remote(
            away.at[side], from_core.at[side], core_send.at[side], core_recv.at[side], (f, xi * 2 + 1 - core)
        )

    order = (lax.rem(xi + 1, 2), xi)
    for place in range(2):
        def store(lo, value, place=place):
            away[place, :, lo : lo + value.shape[1]] = value.astype(jnp.bfloat16)

        project(order[place] * 2 + 1 - core, store)
        core_copy(place).start()

    for place in range(2):
        def store(lo, value, place=place):
            kept[place, :, lo : lo + value.shape[1]] = value

        project(order[place] * 2 + core, store)
    half = tokens // 2

    def plane_copy(dx, dy):
        slot = dx * 2 + dy - 1
        return remote(
            plane_out.at[slot], from_plane.at[slot], plane_send.at[slot], plane_recv.at[slot],
            (fz * 2 + lax.rem(fy + dy, 2), lax.rem(xi + dx, 2) * 2 + core),
        )

    core_copy(0).wait_recv()
    for dy in (1, 0):
        rows = pl.ds(pl.multiple_of(lax.rem(fy + dy, 2) * half, 16), half)
        plane_out[2 + dy - 1] = (
            kept[0, rows, :] + from_core[0, rows, :].astype(jnp.float32)
        ).astype(jnp.bfloat16)
        plane_copy(1, dy).start()
    core_copy(1).wait_recv()
    rows = pl.ds(pl.multiple_of(lax.rem(fy + 1, 2) * half, 16), half)
    plane_out[0] = (kept[1, rows, :] + from_core[1, rows, :].astype(jnp.float32)).astype(jnp.bfloat16)
    plane_copy(0, 1).start()
    rows = pl.ds(pl.multiple_of(fy * half, 16), half)
    own = kept[1, rows, :] + from_core[1, rows, :].astype(jnp.float32)
    plane_copy(0, 1).wait_recv()
    own = own + from_plane[0].astype(jnp.float32)
    plane_copy(1, 0).wait_recv()
    own = own + from_plane[1].astype(jnp.float32)
    plane_copy(1, 1).wait_recv()
    own = own + from_plane[2].astype(jnp.float32)
    block = half // lines
    kept[0, :half, :] = own
    line_out[...] = own.astype(jnp.bfloat16).reshape(line_out.shape)

    def line_copy(step):
        other = lax.rem(fz + step, lines)
        return remote(
            line_out.at[other], from_line.at[step - 1], line_send.at[step - 1], line_recv.at[step - 1],
            (other * 2 + fy, t),
        )

    for step in range(1, lines):
        line_copy(step).start()
    result = kept[0, pl.ds(pl.multiple_of(fz * block, 16), block), :]
    for step in range(1, lines):
        line_copy(step).wait_recv()
        result = result + from_line[step - 1].astype(jnp.float32)
    attend_rows(
        result, q_cols, kv_cols, lengths, cosine, sine_part, keys, values, key_copies, value_copies,
        parts.at[core, xi, fy, fz],
    )
    near = fsdp_count // tp_count
    def aline_copy(step, source):
        other = lax.rem(fz + step, lines)
        spot = parts.at[core, xi, fy, source]
        return remote(spot, spot, aline_send.at[step - 1], aline_recv.at[step - 1], (other * 2 + fy, t))

    def aplane_copy(dx, dy, step, back):
        slot = dx * 2 + dy - 1
        other_x, other_y = lax.rem(xi + dx, 2), lax.rem(fy + dy, 2)
        piece = lax.rem(fz - step + lines, lines)
        spot = parts.at[core, other_x, other_y, piece] if back else parts.at[core, xi, fy, piece]
        return remote(
            spot, spot, aplane_send.at[slot, step], aplane_recv.at[slot, step],
            (fz * 2 + other_y, other_x * 2 + core),
        )

    def acore_copy(dx, dy, back):
        slot = dx * 2 + dy
        side = 1 - core if back else core
        spot = parts.at[side, lax.rem(xi + dx, 2), lax.rem(fy + dy, 2)]
        return remote(spot, spot, acore_send.at[slot], acore_recv.at[slot], (f, xi * 2 + 1 - core))

    for step in range(1, lines):
        aline_copy(step, fz).start()
    peers = ((1, 1), (1, 0), (0, 1))
    for step in range(lines):
        if step > 0:
            aline_copy(step, lax.rem(fz - step + lines, lines)).wait_recv()
        for dx, dy in peers:
            aplane_copy(dx, dy, step, False).start()
    acore_copy(0, 0, False).start()
    for dx, dy in reversed(peers):
        for step in range(lines):
            aplane_copy(dx, dy, step, True).wait_recv()
        acore_copy(dx, dy, False).start()
    weight_copy.wait()
    cols = w_buf.shape[1] // tp_count

    def add(side, far, first):
        columns = pl.ds(pl.multiple_of((far * 2 + side) * cols, 128), cols)
        value = contract_last(parts[side, far].reshape(tokens, cols), w_buf[:, columns])
        if first:
            sums[...] = value
        else:
            sums[...] += value

    add(core, xi, True)
    add(core, lax.rem(xi + 1, 2), False)
    for dx, dy in ((0, 0),) + tuple(reversed(peers)):
        acore_copy(dx, dy, True).wait_recv()
    add(1 - core, xi, False)
    add(1 - core, lax.rem(xi + 1, 2), False)
    blocks[...] = sums[...].astype(jnp.bfloat16).reshape(blocks.shape)
    target = f // near
    place = lax.rem(f, near) * tp_count + t

    def out_copy(step):
        other = lax.rem(f + step, fsdp_count)
        return remote(
            blocks.at[lax.rem(other, 2) * lines + other // 2], gathered.at[place],
            out_send.at[step], out_recv.at[place], (other, target),
        )

    for step in range(1, fsdp_count):
        out_copy(step).start()

    @pl.when(target != t)
    def _():
        out_copy(0).start()

    @pl.when(target == t)
    def _():
        gathered[place] = blocks[fy * lines + fz]

    def source(slot):
        return t * near + slot // tp_count, slot % tp_count

    for slot in range(near * tp_count):
        sender_f, sender_t = source(slot)

        @pl.when(jnp.logical_or(sender_f != f, sender_t != t))
        def _(slot=slot, sender_f=sender_f, sender_t=sender_t):
            remote(
                blocks.at[0], gathered.at[slot], out_send.at[0], out_recv.at[slot], (sender_f, sender_t)
            ).wait_recv()

    got[...] = gathered[...]
    for step in range(1, lines):
        aline_copy(step, fz).wait_send()
    for dx, dy in peers:
        for step in range(lines):
            aplane_copy(dx, dy, step, False).wait_send()
    for dx, dy in ((0, 0),) + peers:
        acore_copy(dx, dy, False).wait_send()
    for step in range(1, fsdp_count):
        out_copy(step).wait_send()

    @pl.when(target != t)
    def _():
        out_copy(0).wait_send()
    for step in range(1, tp_count):
        x_copy(step).wait_send()

    def done_sq(step, carry):
        sq_copy(step).wait_send()
        return carry

    lax.fori_loop(1, count, done_sq, 0)
    for place in range(2):
        core_copy(place).wait_send()
    plane_copy(0, 1).wait_send()
    plane_copy(1, 0).wait_send()
    plane_copy(1, 1).wait_send()
    for step in range(1, lines):
        line_copy(step).wait_send()


def block(
    fsdp_count, tp_count, lengths, picked, squares, gain, cosine, sine_part, w_query, w_keyval, w_out,
    key_cache, value_cache
):
    _, tokens, depth = picked.shape
    count = fsdp_count * tp_count
    lines = fsdp_count // 2
    cols = (w_query.shape[1] + w_keyval.shape[1]) // tp_count
    half = tokens // 2
    row_tokens = tokens // fsdp_count
    out_cols = w_out.shape[1] // tp_count
    slots = fsdp_count // tp_count * tp_count
    dma = pltpu.SemaphoreType.DMA
    bf16, f32 = jnp.bfloat16, jnp.float32
    vmem = pl.BlockSpec(memory_space=pltpu.VMEM)
    hbm = pl.BlockSpec(memory_space=pltpu.HBM)
    return pl.pallas_call(
        functools.partial(block_kernel, fsdp_count, tp_count),
        out_shape=jax.ShapeDtypeStruct((slots, row_tokens, depth), bf16),
        in_specs=[pl.BlockSpec(memory_space=pltpu.SMEM)] + [vmem] * 5 + [hbm] * 5,
        out_specs=vmem,
        scratch_shapes=[
            pltpu.VMEM(w_query.shape, bf16),
            pltpu.VMEM(w_keyval.shape, bf16),
            pltpu.VMEM((tp_count - 1, tokens, depth), bf16),
            pltpu.VMEM((count - 1,) + squares.shape, f32),
            pltpu.VMEM((2, tokens, cols), bf16),
            pltpu.VMEM((2, tokens, cols), f32),
            pltpu.VMEM((2, tokens, cols), bf16),
            pltpu.VMEM((3, half, cols), bf16),
            pltpu.VMEM((3, half, cols), bf16),
            pltpu.VMEM((lines, half // lines, cols), bf16),
            pltpu.VMEM((lines - 1, half // lines, cols), bf16),
            pltpu.VMEM(w_out.shape, bf16),
            pltpu.VMEM((2, 2, 2, lines, row_tokens, out_cols), bf16),
            pltpu.VMEM((tokens, depth), f32),
            pltpu.VMEM((fsdp_count, row_tokens, depth), bf16),
            pltpu.VMEM((slots, row_tokens, depth), bf16),
            pltpu.VMEM(key_cache.shape, bf16),
            pltpu.VMEM(value_cache.shape, bf16),
            dma((3,)), dma((2, key_cache.shape[0])),
            dma((tp_count - 1,)), dma((tp_count - 1,)),
            dma((count - 1,)), dma((count - 1,)),
            dma((2,)), dma((2,)),
            dma((3,)), dma((3,)),
            dma((lines - 1,)), dma((lines - 1,)),
            dma((lines - 1,)), dma((lines - 1,)),
            dma((3, lines)), dma((3, lines)),
            dma((4,)), dma((4,)),
            dma((fsdp_count,)), dma((slots,)),
        ],
        compiler_params=pltpu.CompilerParams(
            collective_id=0, has_side_effects=True, vmem_limit_bytes=VMEM_LIMIT
        ),
        name="block",
    )(
        lengths, picked, squares, gain, cosine, sine_part, w_query, w_keyval, w_out, key_cache, value_cache
    )


def on_device(
    token_ids, lengths, embedding, norm_gain, w_query, w_keyval, w_out, key_cache, value_cache
):
    tp_count = lax.axis_size("tp")
    fsdp_count = lax.axis_size("fsdp")
    tp_rank = lax.axis_index("tp")
    fsdp_rank = lax.axis_index("fsdp")
    step_count = token_ids.shape[1]
    row_dev = lengths.shape[0]
    vocab_part = embedding.shape[0]
    token_count = token_ids.size
    depth = w_query.shape[0]
    ordered = token_ids.reshape(fsdp_count // 2, 2, -1).transpose(1, 0, 2).reshape(-1)
    shifted = ordered - tp_rank * vocab_part
    picked = embedding.at[shifted].get(mode="fill", fill_value=0, wrap_negative_indices=False)
    wide = picked.astype(jnp.float32)
    squares = jnp.broadcast_to(jnp.sum(wide * wide, -1)[None, :], (8, token_count))
    picked = picked.reshape(token_count, tp_count, depth).transpose(1, 0, 2)
    gain = lax.dynamic_slice(norm_gain, ((fsdp_rank * tp_count + tp_rank) * depth,), (depth,))
    positions = (lengths[:, None] + jnp.arange(step_count, dtype=jnp.int32)[None, :]).reshape(-1)
    midpoint = HD // 2
    frequency = ROPE_BASE ** (-2.0 * jnp.arange(midpoint, dtype=jnp.float32) / HD)
    angles = positions.astype(jnp.float32)[:, None] * frequency
    cosine = jnp.cos(angles)
    sine_part = jnp.sin(angles)
    rows = block(
        fsdp_count, tp_count, lengths, picked, squares, gain[None, :],
        jnp.concatenate([cosine, cosine], -1), jnp.concatenate([-sine_part, sine_part], -1),
        w_query, w_keyval, w_out, key_cache, value_cache,
    )
    return rows.transpose(1, 0, 2).reshape(row_dev, step_count, -1)


def solution(mesh):
    return jax.shard_map(
        on_device,
        mesh=mesh,
        in_specs=(
            P(),
            P("fsdp"),
            P("tp", "fsdp"),
            P(),
            P(("fsdp", "tp"), None),
            P(("fsdp", "tp"), None),
            P(("fsdp", "tp"), None),
            P("fsdp", None, "tp"),
            P("fsdp", None, "tp"),
        ),
        out_specs=P("fsdp", None, "tp"),
        check_vma=False,
    )
```
